32 devices in a mesh: grp: 4 (over y, core), blk: 8 (over z, x).
Axes of the slice: x: 2, y: 2, z: 4, core: 2. Of those that a mesh axis runs over, the one named last changes fastest.
Arguments:
- images: float32 [12288, 1152], P(('grp', 'blk')), may hold values from -6 to 6
- texts: float32 [12288, 1152], P(('grp', 'blk')), may hold values from -6 to 6
- pair_index: int32 [32, 384], P(('grp', 'blk')), may hold values from 0 to 383, each once within a row
Outputs:
- row_loss: float32 [12288], P(('grp', 'blk'))
- image_grad: float32 [12288, 1152], P(('grp', 'blk'))
- text_grad: float32 [12288, 1152], P(('grp', 'blk'))
The draws below stay inside these ranges and needn't reach their ends.
Inputs may be any that keep to these rules, and one draw needn't show every extreme that they name: Each row of pair_index is a permutation of 0 to 383.
All inputs are finite; a program needn't handle non-finite values.
Results may differ from the reference program's by a relative error of at most 0.0001.
Values sent between devices are 32-bit elements; how exact they have to be, the bound alone decides.
A program may use at most 64 MiB of HBM per device.

```python
import jax
import jax.numpy as jnp
from jax import lax

D = 1152
ROWS = 384
BLOCKS = 32
TOTAL = 12288
N_GRP = 4
N_BLK = 8


def steps_of(own_key, shape, cuts, low, top_value):
    level = 1.0
    for dim, blocks in cuts:
        heights = jax.random.uniform(jax.random.fold_in(jax.random.fold_in(own_key, 6), dim), (blocks,), jnp.float32, low / len(cuts), top_value / len(cuts))
        level = level * jnp.repeat(jnp.exp(heights), shape[dim] // blocks).reshape((-1,) + (1,) * (len(shape) - 1 - dim))
    return level


def gaussian(rng, extent, scale, reach, pieces=(), kind=jnp.bfloat16):
    array = jax.random.normal(rng, extent, jnp.float32) * scale
    if len(pieces) > 0:
        array = steps_of(rng, extent, pieces, -0.22, 0.18) * array
    return jnp.clip(array, min=-reach, max=reach).astype(kind)


def setup_inputs(seed: int = 0) -> dict:
    streams_of = jax.random.split(jax.random.key(seed), 4)
    images = gaussian(streams_of[0], (TOTAL, D), 1.0, 6.0, ((0, 32),), jnp.float32)
    texts = gaussian(streams_of[1], (TOTAL, D), 1.0, 6.0, ((0, 32),), jnp.float32)
    pair_index = jax.vmap(lambda own: jax.random.permutation(own, ROWS))(jax.random.split(streams_of[2], BLOCKS)).reshape((BLOCKS, ROWS)).astype(jnp.int32)
    return {"images": images, "texts": texts, "pair_index": pair_index}


def meet(images, texts, positive, scale):
    logits = scale * jnp.einsum('gbrd,gbcd->gbrc', images, texts, precision=lax.Precision.HIGHEST) - 3.0
    weight = jax.nn.sigmoid(logits) - positive
    losses = jnp.sum(jax.nn.softplus(logits) - positive * logits, axis=-1)
    image_part = scale * jnp.einsum('gbrc,gbcd->gbrd', weight, texts, precision=lax.Precision.HIGHEST)
    text_part = scale * jnp.einsum('gbrc,gbrd->gbcd', weight, images, precision=lax.Precision.HIGHEST)
    return losses, image_part, text_part


def reference(images, texts, pair_index):
    scale = 2.0 * D ** -0.5
    blocks_x = images.reshape(N_GRP, N_BLK, ROWS, D)
    blocks_y = texts.reshape(N_GRP, N_BLK, ROWS, D)
    columns = jnp.arange(ROWS, dtype=jnp.int32)
    positive = (pair_index.reshape(N_GRP, N_BLK, ROWS, 1) == columns[None, None, None, :]).astype(jnp.float32)
    nothing = jnp.zeros_like(positive)
    losses, image_grad, text_grad = meet(blocks_x, blocks_y, positive, scale)
    for back in (1, 2):
        seen = jnp.roll(blocks_y, back, axis=1)
        more_loss, image_part, text_part = meet(blocks_x, seen, nothing, scale)
        losses = losses + more_loss
        image_grad = image_grad + image_part
        text_grad = text_grad + jnp.roll(text_part, -back, axis=1)
    seen = jnp.roll(blocks_y, -1, axis=0)
    more_loss, image_part, text_part = meet(blocks_x, seen, nothing, scale)
    losses = losses + more_loss
    image_grad = image_grad + image_part
    text_grad = text_grad + jnp.roll(text_part, 1, axis=0)
    row_loss = (losses / (4.0 * ROWS)).reshape(TOTAL)
    return row_loss, image_grad.reshape(TOTAL, D), text_grad.reshape(TOTAL, D)
```

```python
import functools

import jax
import jax.numpy as jnp
from jax import lax
from jax.experimental import pallas as pl
from jax.experimental.pallas import tpu as pltpu
from jax.sharding import PartitionSpec as P

MESH = pl.DeviceIdType.MESH
CHUNK = 128
PIECE = 64
PARTS = CHUNK // PIECE

GROUP, FAR, NEAR = 0, 1, 2


def split(value):
    high = value.astype(jnp.bfloat16)
    return high, (value - high.astype(jnp.float32)).astype(jnp.bfloat16)


def across(left, right):
    return lax.dot_general(left, right, (((1,), (1,)), ((), ())), preferred_element_type=jnp.float32)


def kernel(
    n_grp, n_blk, scale,
    img, txt, pair, loss_out, img_out, txt_out,
    land, own, high, low, acc, match, total,
    own_sem, out_sem, send_sem, relay_sem, recv_sem,
):
    rows, width = img.shape
    pieces = rows // PIECE
    chunks = rows // CHUNK
    g, i = lax.axis_index("grp"), lax.axis_index("blk")
    odd = lax.rem(i, 2)
    relayed = 1 - odd
    partner = (g, i + 1 - 2 * odd)
    ahead, behind = (g, lax.rem(i + 2, n_blk)), (g, lax.rem(i + n_blk - 2, n_blk))
    upper, lower = (lax.rem(g + 1, n_grp), i), (lax.rem(g + n_grp - 1, n_grp), i)

    loads = [
        pltpu.make_async_copy(img, own.at[0], own_sem.at[0]),
        pltpu.make_async_copy(txt, own.at[1], own_sem.at[1]),
    ]
    for load in loads:
        load.start()

    barrier = pltpu.get_barrier_semaphore()
    for device in (partner, ahead, behind, upper, lower):
        pl.semaphore_signal(barrier, inc=1, device_id=device, device_id_type=MESH)
    pl.semaphore_wait(barrier, 5)

    def span(q):
        return pl.ds(pl.multiple_of(q * PIECE, PIECE), PIECE)

    def send(src, slot, q, lane, device):
        return pltpu.make_async_remote_copy(
            src_ref=src.at[span(q)],
            dst_ref=land.at[slot, span(q)],
            send_sem=send_sem.at[lane, q],
            recv_sem=recv_sem.at[slot, q],
            device_id=device,
            device_id_type=MESH,
        )

    def relay(q):
        return pltpu.make_async_remote_copy(
            src_ref=land.at[2 * FAR + relayed, span(q)],
            dst_ref=land.at[2 * NEAR + relayed, span(q)],
            send_sem=relay_sem.at[q],
            recv_sem=recv_sem.at[2 * NEAR + relayed, q],
            device_id=partner,
            device_id_type=MESH,
        )

    def arrived(slot, q):
        pltpu.make_async_remote_copy(
            src_ref=land.at[slot, span(q)],
            dst_ref=land.at[slot, span(q)],
            send_sem=relay_sem.at[q],
            recv_sem=recv_sem.at[slot, q],
            device_id=partner,
            device_id_type=MESH,
        ).wait_recv()

    def send_all(q, _):
        send(txt, 2 * FAR, q, 0, ahead).start()
        send(img, 2 * FAR + 1, q, 1, behind).start()

        @pl.when(odd == 0)
        def _():
            send(txt, 2 * NEAR, q, 2, partner).start()

        @pl.when(odd == 1)
        def _():
            send(img, 2 * NEAR + 1, q, 2, partner).start()

        send(txt, 2 * GROUP, q, 3, lower).start()
        send(img, 2 * GROUP + 1, q, 4, upper).start()
        return 0

    lax.fori_loop(0, pieces, send_all, 0)

    for load in loads:
        load.wait()
    for kind in range(2):
        for c in range(chunks):
            at = pl.ds(c * CHUNK, CHUNK)
            high[kind, at], low[kind, at] = split(own[kind, at])
    index = pair[...]
    by_row = jnp.transpose(
        jnp.broadcast_to(index.astype(jnp.float32), (CHUNK, rows))
    )
    lane = lax.broadcasted_iota(jnp.int32, (rows, CHUNK), 1).astype(jnp.float32)
    row = lax.broadcasted_iota(jnp.int32, (rows, CHUNK), 0)
    for c in range(chunks):
        match[0, c] = (by_row == lane + float(c * CHUNK)).astype(jnp.float32)
        match[1, c] = (row == index[:, c * CHUNK : (c + 1) * CHUNK]).astype(jnp.float32)
    acc[...] = jnp.zeros_like(acc)
    total[...] = jnp.zeros_like(total)

    def meet(kind, their_high, their_low, positive):
        both = across(high[kind], jnp.concatenate([their_high, their_low], axis=0))
        dots = both[:, :CHUNK] + both[:, CHUNK:] + across(low[kind], their_high)
        s = scale * dots - 3.0
        e = jnp.exp(-jnp.abs(s))
        weight = jnp.where(s >= 0.0, 1.0, e) / (1.0 + e)
        if positive is not None:
            weight = weight - positive
        if kind == 0:
            loss = jnp.maximum(s, 0.0) + jnp.log1p(e)
            if positive is not None:
                loss = loss - positive * s
            total[...] += loss
        w_high, w_low = split(scale * weight)
        w_both = jnp.concatenate([w_high, w_low], axis=1)
        for t in range(0, width, 384):
            cut = slice(t, min(t + 384, width))
            top = their_high[:, cut]
            acc[kind, :, cut] += jnp.dot(
                w_both, jnp.concatenate([top, top], axis=0), preferred_element_type=jnp.float32
            ) + jnp.dot(w_high, their_low[:, cut], preferred_element_type=jnp.float32)

    def own_step(c, _):
        at = pl.ds(pl.multiple_of(c * CHUNK, CHUNK), CHUNK)
        for kind in range(2):
            meet(kind, high[1 - kind, at], low[1 - kind, at], match[kind, c])
        return 0

    lax.fori_loop(0, chunks, own_step, 0)

    def step(n, _):
        c, m = n // 3, n % 3
        for h in range(PARTS):
            q = c * PARTS + h
            arrived(2 * m + relayed, q)

            @pl.when(m == FAR)
            def _():
                relay(q).start()

        for h in range(PARTS):
            arrived(2 * m + odd, c * PARTS + h)
        at = pl.ds(pl.multiple_of(c * CHUNK, CHUNK), CHUNK)
        for kind in range(2):
            meet(kind, *split(land[2 * m + kind, at]), None)
        return 0

    lax.fori_loop(0, 3 * chunks, step, 0)

    stores = [
        pltpu.make_async_copy(acc.at[0], img_out, out_sem.at[0]),
        pltpu.make_async_copy(acc.at[1], txt_out, out_sem.at[1]),
    ]
    for store in stores:
        store.start()
    loss_out[...] = jnp.sum(jnp.transpose(total[...]), axis=0, keepdims=True) / (4.0 * rows)

    def drain(q, _):
        for line, device in enumerate((ahead, behind, partner, lower, upper)):
            send(txt, 0, q, line, device).wait_send()
        relay(q).wait_send()
        return 0

    lax.fori_loop(0, pieces, drain, 0)
    for store in stores:
        store.wait()


def on_device(n_grp, n_blk, images, texts, pair_index):
    rows, width = images.shape
    scale = 2.0 * width ** (-0.5)
    pieces = rows // PIECE
    any_space = pl.BlockSpec(memory_space=pl.ANY)
    vmem = pl.BlockSpec(memory_space=pltpu.VMEM)
    block = jax.ShapeDtypeStruct((rows, width), jnp.float32)
    loss, image_grad, text_grad = pl.pallas_call(
        functools.partial(kernel, n_grp, n_blk, scale),
        out_shape=(jax.ShapeDtypeStruct((1, rows), jnp.float32), block, block),
        in_specs=[any_space, any_space, vmem],
        out_specs=(vmem, any_space, any_space),
        scratch_shapes=[
            pltpu.VMEM((6, rows, width), jnp.float32),
            pltpu.VMEM((2, rows, width), jnp.float32),
            pltpu.VMEM((2, rows, width), jnp.bfloat16),
            pltpu.VMEM((2, rows, width), jnp.bfloat16),
            pltpu.VMEM((2, rows, width), jnp.float32),
            pltpu.VMEM((2, rows // CHUNK, rows, CHUNK), jnp.float32),
            pltpu.VMEM((rows, CHUNK), jnp.float32),
            pltpu.SemaphoreType.DMA((2,)),
            pltpu.SemaphoreType.DMA((2,)),
            pltpu.SemaphoreType.DMA((5, pieces)),
            pltpu.SemaphoreType.DMA((pieces,)),
            pltpu.SemaphoreType.DMA((6, pieces)),
        ],
        compiler_params=pltpu.CompilerParams(
            collective_id=0, has_side_effects=True, vmem_limit_bytes=52 * 1024 * 1024
        ),
        cost_estimate=pl.CostEstimate(
            flops=16 * 3 * 2 * rows * rows * width,
            bytes_accessed=4 * 4 * rows * width,
            transcendentals=8 * rows * rows,
        ),
    )(images, texts, pair_index)
    return loss.reshape(rows), image_grad, text_grad


def solution(mesh):
    n_grp, n_blk = mesh.shape["grp"], mesh.shape["blk"]
    assert n_blk % 2 == 0
    in_specs = (P(("grp", "blk"), None), P(("grp", "blk"), None), P(("grp", "blk"), None))
    out_specs = (P(("grp", "blk")), P(("grp", "blk"), None), P(("grp", "blk"), None))
    return jax.shard_map(
        functools.partial(on_device, n_grp, n_blk),
        mesh=mesh, in_specs=in_specs, out_specs=out_specs, check_vma=False,
    )
```

```python
import functools

import jax
import jax.numpy as jnp
from jax import lax
from jax.experimental import pallas as pl
from jax.experimental.pallas import tpu as pltpu
from jax.sharding import PartitionSpec as P

MESH = pl.DeviceIdType.MESH
CHUNK = 128
PIECE = 64
PARTS = CHUNK // PIECE

GROUP, FAR, NEAR = 0, 1, 2


def split(value):
    high = value.astype(jnp.bfloat16)
    return high, (value - high.astype(jnp.float32)).astype(jnp.bfloat16)


def across(left, right):
    return lax.dot_general(left, right, (((1,), (1,)), ((), ())), preferred_element_type=jnp.float32)


def kernel(
    n_grp, n_blk, scale,
    img, txt, pair, loss_out, img_out, txt_out,
    land, own, high, low, acc, match, total,
    own_sem, out_sem, send_sem, relay_sem, recv_sem,
):
    rows, width = img.shape
    pieces = rows // PIECE
    chunks = rows // CHUNK
    g, i = lax.axis_index("grp"), lax.axis_index("blk")
    odd = lax.rem(i, 2)
    relayed = 1 - odd
    partner = (g, i + 1 - 2 * odd)
    ahead, behind = (g, lax.rem(i + 2, n_blk)), (g, lax.rem(i + n_blk - 2, n_blk))
    upper, lower = (lax.rem(g + 1, n_grp), i), (lax.rem(g + n_grp - 1, n_grp), i)

    loads = [
        pltpu.make_async_copy(img, own.at[0], own_sem.at[0]),
        pltpu.make_async_copy(txt, own.at[1], own_sem.at[1]),
    ]
    for load in loads:
        load.start()

    barrier = pltpu.get_barrier_semaphore()
    for device in (partner, ahead, behind, upper, lower):
        pl.semaphore_signal(barrier, inc=1, device_id=device, device_id_type=MESH)
    pl.semaphore_wait(barrier, 5)

    def span(q):
        return pl.ds(pl.multiple_of(q * PIECE, PIECE), PIECE)

    def send(src, slot, q, lane, device):
        return pltpu.make_async_remote_copy(
            src_ref=src.at[span(q)],
            dst_ref=land.at[slot, span(q)],
            send_sem=send_sem.at[lane, q],
            recv_sem=recv_sem.at[slot, q],
            device_id=device,
            device_id_type=MESH,
        )

    def relay(q):
        return pltpu.make_async_remote_copy(
            src_ref=land.at[2 * FAR + relayed, span(q)],
            dst_ref=land.at[2 * NEAR + relayed, span(q)],
            send_sem=relay_sem.at[q],
            recv_sem=recv_sem.at[2 * NEAR + relayed, q],
            device_id=partner,
            device_id_type=MESH,
        )

    def arrived(slot, q):
        pltpu.make_async_remote_copy(
            src_ref=land.at[slot, span(q)],
            dst_ref=land.at[slot, span(q)],
            send_sem=relay_sem.at[q],
            recv_sem=recv_sem.at[slot, q],
            device_id=partner,
            device_id_type=MESH,
        ).wait_recv()

    def send_first(q, _):
        @pl.when(odd == 0)
        def _():
            send(img, 2 * FAR + 1, q, 0, behind).start()
            send(txt, 2 * NEAR, q, 2, partner).start()

        @pl.when(odd == 1)
        def _():
            send(txt, 2 * FAR, q, 0, ahead).start()
            send(img, 2 * NEAR + 1, q, 2, partner).start()

        send(txt, 2 * GROUP, q, 3, lower).start()
        return 0

    def send_second(q, _):
        @pl.when(odd == 0)
        def _():
            send(txt, 2 * FAR, q, 1, ahead).start()

        @pl.when(odd == 1)
        def _():
            send(img, 2 * FAR + 1, q, 1, behind).start()

        send(img, 2 * GROUP + 1, q, 4, upper).start()
        return 0

    lax.fori_loop(0, pieces, send_first, 0)
    lax.fori_loop(0, pieces, send_second, 0)

    for load in loads:
        load.wait()
    for kind in range(2):
        for c in range(chunks):
            at = pl.ds(c * CHUNK, CHUNK)
            high[kind, at], low[kind, at] = split(own[kind, at])
    index = pair[...]
    by_row = jnp.transpose(
        jnp.broadcast_to(index.astype(jnp.float32), (CHUNK, rows))
    )
    lane = lax.broadcasted_iota(jnp.int32, (rows, CHUNK), 1).astype(jnp.float32)
    row = lax.broadcasted_iota(jnp.int32, (rows, CHUNK), 0)
    for c in range(chunks):
        match[0, c] = (by_row == lane + float(c * CHUNK)).astype(jnp.float32)
        match[1, c] = (row == index[:, c * CHUNK : (c + 1) * CHUNK]).astype(jnp.float32)
    acc[...] = jnp.zeros_like(acc)
    total[...] = jnp.zeros_like(total)

    def meet(kind, their_high, their_low, positive):
        both = across(high[kind], jnp.concatenate([their_high, their_low], axis=0))
        dots = both[:, :CHUNK] + both[:, CHUNK:] + across(low[kind], their_high)
        s = scale * dots - 3.0
        e = jnp.exp(-jnp.abs(s))
        weight = jnp.where(s >= 0.0, 1.0, e) / (1.0 + e)
        if positive is not None:
            weight = weight - positive

        @pl.when(kind == 0)
        def _():
            loss = jnp.maximum(s, 0.0) + jnp.log1p(e)
            if positive is not None:
                loss = loss - positive * s
            total[...] += loss

        w_high, w_low = split(scale * weight)
        w_both = jnp.concatenate([w_high, w_low], axis=1)
        for t in range(0, width, 384):
            cut = slice(t, min(t + 384, width))
            top = their_high[:, cut]
            acc[kind, :, cut] += jnp.dot(
                w_both, jnp.concatenate([top, top], axis=0), preferred_element_type=jnp.float32
            ) + jnp.dot(w_high, their_low[:, cut], preferred_element_type=jnp.float32)

    def own_step(n, _):
        c, kind = n // 2, n % 2
        at = pl.ds(pl.multiple_of(c * CHUNK, CHUNK), CHUNK)
        meet(kind, high[1 - kind, at], low[1 - kind, at], match[kind, c])
        return 0

    lax.fori_loop(0, 2 * chunks, own_step, 0)

    def visit(pair_of, kind, c):
        slot = 2 * pair_of + kind
        at = pl.ds(pl.multiple_of(c * CHUNK, CHUNK), CHUNK)
        meet(kind, *split(land[slot, at]), None)

    def early(n, _):
        c, j = n // 4, n % 4
        pair_of = (1 - (j + 2) // 3) * FAR + (j // 3) * NEAR
        second = (j // 2) * (1 - j // 3)
        kind = relayed + second * (odd - relayed)
        for h in range(PARTS):
            q = c * PARTS + h
            arrived(2 * pair_of + kind, q)

            @pl.when(j == 0)
            def _():
                relay(q).start()

        visit(pair_of, kind, c)
        return 0

    lax.fori_loop(0, 4 * chunks, early, 0)

    def store(kind, out):
        return pltpu.make_async_copy(acc.at[kind], out, out_sem.at[kind])

    @pl.when(odd == 0)
    def _():
        store(1, txt_out).start()

    @pl.when(odd == 1)
    def _():
        store(0, img_out).start()

    def late(n, _):
        c, pair_of = n // 2, FAR + n % 2
        for h in range(PARTS):
            arrived(2 * pair_of + odd, c * PARTS + h)
        visit(pair_of, odd, c)
        return 0

    lax.fori_loop(0, 2 * chunks, late, 0)

    @pl.when(odd == 0)
    def _():
        store(0, img_out).start()

    @pl.when(odd == 1)
    def _():
        store(1, txt_out).start()

    loss_out[...] = jnp.sum(jnp.transpose(total[...]), axis=0, keepdims=True) / (4.0 * rows)

    def drain(q, _):
        for line, device in enumerate((ahead, behind, partner, lower, upper)):
            send(txt, 0, q, line, device).wait_send()
        relay(q).wait_send()
        return 0

    lax.fori_loop(0, pieces, drain, 0)
    store(0, img_out).wait()
    store(1, txt_out).wait()


def on_device(n_grp, n_blk, images, texts, pair_index):
    rows, width = images.shape
    scale = 2.0 * width ** (-0.5)
    pieces = rows // PIECE
    any_space = pl.BlockSpec(memory_space=pl.ANY)
    vmem = pl.BlockSpec(memory_space=pltpu.VMEM)
    block = jax.ShapeDtypeStruct((rows, width), jnp.float32)
    loss, image_grad, text_grad = pl.pallas_call(
        functools.partial(kernel, n_grp, n_blk, scale),
        out_shape=(jax.ShapeDtypeStruct((1, rows), jnp.float32), block, block),
        in_specs=[any_space, any_space, vmem],
        out_specs=(vmem, any_space, any_space),
        scratch_shapes=[
            pltpu.VMEM((6, rows, width), jnp.float32),
            pltpu.VMEM((2, rows, width), jnp.float32),
            pltpu.VMEM((2, rows, width), jnp.bfloat16),
            pltpu.VMEM((2, rows, width), jnp.bfloat16),
            pltpu.VMEM((2, rows, width), jnp.float32),
            pltpu.VMEM((2, rows // CHUNK, rows, CHUNK), jnp.float32),
            pltpu.VMEM((rows, CHUNK), jnp.float32),
            pltpu.SemaphoreType.DMA((2,)),
            pltpu.SemaphoreType.DMA((2,)),
            pltpu.SemaphoreType.DMA((5, pieces)),
            pltpu.SemaphoreType.DMA((pieces,)),
            pltpu.SemaphoreType.DMA((6, pieces)),
        ],
        compiler_params=pltpu.CompilerParams(
            collective_id=0, has_side_effects=True, vmem_limit_bytes=60 * 1024 * 1024
        ),
        cost_estimate=pl.CostEstimate(
            flops=16 * 3 * 2 * rows * rows * width,
            bytes_accessed=4 * 4 * rows * width,
            transcendentals=8 * rows * rows,
        ),
    )(images, texts, pair_index)
    return loss.reshape(rows), image_grad, text_grad


def solution(mesh):
    n_grp, n_blk = mesh.shape["grp"], mesh.shape["blk"]
    assert n_blk % 2 == 0
    in_specs = (P(("grp", "blk"), None), P(("grp", "blk"), None), P(("grp", "blk"), None))
    out_specs = (P(("grp", "blk")), P(("grp", "blk"), None), P(("grp", "blk"), None))
    return jax.shard_map(
        functools.partial(on_device, n_grp, n_blk),
        mesh=mesh, in_specs=in_specs, out_specs=out_specs, check_vma=False,
    )
```

```python
import functools

import jax
import jax.numpy as jnp
from jax import lax
from jax.experimental import pallas as pl
from jax.experimental.pallas import tpu as pltpu
from jax.sharding import PartitionSpec as P

MESH = pl.DeviceIdType.MESH
CHUNK = 128
PIECE = 64
PARTS = CHUNK // PIECE
STRIPS = 2

GROUP, FAR, NEAR = 0, 1, 2


def split(value):
    high = value.astype(jnp.bfloat16)
    return high, (value - high.astype(jnp.float32)).astype(jnp.bfloat16)


def across(left, right):
    return lax.dot_general(left, right, (((1,), (1,)), ((), ())), preferred_element_type=jnp.float32)


def kernel(
    n_grp, n_blk, scale,
    img, txt, pair_in, loss_out, img_out, txt_out,
    pair, loss_row, land, own, high, low, acc, match, total,
    own_sem, out_sem, send_sem, relay_sem, recv_sem,
):
    rows, width = img.shape
    pieces = rows // PIECE
    chunks = rows // CHUNK
    g, i = lax.axis_index("grp"), lax.axis_index("blk")
    odd = lax.rem(i, 2)
    relayed = 1 - odd
    partner = (g, i + 1 - 2 * odd)
    ahead, behind = (g, lax.rem(i + 2, n_blk)), (g, lax.rem(i + n_blk - 2, n_blk))
    upper, lower = (lax.rem(g + 1, n_grp), i), (lax.rem(g + n_grp - 1, n_grp), i)

    loads = [
        pltpu.make_async_copy(img, own.at[0], own_sem.at[0]),
        pltpu.make_async_copy(txt, own.at[1], own_sem.at[1]),
        pltpu.make_async_copy(pair_in, pair, own_sem.at[2]),
    ]
    for load in loads:
        load.start()

    barrier = pltpu.get_barrier_semaphore()
    for device in (partner, ahead, behind, upper, lower):
        pl.semaphore_signal(barrier, inc=1, device_id=device, device_id_type=MESH)
    pl.semaphore_wait(barrier, 5)

    def span(q):
        return pl.ds(pl.multiple_of(q * PIECE, PIECE), PIECE)

    def send(src, slot, q, lane, device):
        return pltpu.make_async_remote_copy(
            src_ref=src.at[span(q)],
            dst_ref=land.at[slot, span(q)],
            send_sem=send_sem.at[lane, q],
            recv_sem=recv_sem.at[slot, q],
            device_id=device,
            device_id_type=MESH,
        )

    def relay(q):
        return pltpu.make_async_remote_copy(
            src_ref=land.at[2 * FAR + relayed, span(q)],
            dst_ref=land.at[2 * NEAR + relayed, span(q)],
            send_sem=relay_sem.at[q],
            recv_sem=recv_sem.at[2 * NEAR + relayed, q],
            device_id=partner,
            device_id_type=MESH,
        )

    def arrived(slot, q):
        pltpu.make_async_remote_copy(
            src_ref=land.at[slot, span(q)],
            dst_ref=land.at[slot, span(q)],
            send_sem=relay_sem.at[q],
            recv_sem=recv_sem.at[slot, q],
            device_id=partner,
            device_id_type=MESH,
        ).wait_recv()

    def send_first(q, _):
        @pl.when(odd == 0)
        def _():
            send(img, 2 * FAR + 1, q, 0, behind).start()
            send(txt, 2 * NEAR, q, 2, partner).start()

        @pl.when(odd == 1)
        def _():
            send(txt, 2 * FAR, q, 0, ahead).start()
            send(img, 2 * NEAR + 1, q, 2, partner).start()

        send(txt, 2 * GROUP, q, 3, lower).start()
        return 0

    def send_second(q, _):
        @pl.when(odd == 0)
        def _():
            send(txt, 2 * FAR, q, 1, ahead).start()

        @pl.when(odd == 1)
        def _():
            send(img, 2 * FAR + 1, q, 1, behind).start()

        send(img, 2 * GROUP + 1, q, 4, upper).start()
        return 0

    lax.fori_loop(0, pieces, send_first, 0)
    lax.fori_loop(0, pieces, send_second, 0)

    for load in loads:
        load.wait()
    for kind in range(2):
        for c in range(chunks):
            at = pl.ds(c * CHUNK, CHUNK)
            high[kind, at], low[kind, at] = split(own[kind, at])
    index = pair[...]
    by_row = jnp.transpose(
        jnp.broadcast_to(index.astype(jnp.float32), (CHUNK, rows))
    )
    lane = lax.broadcasted_iota(jnp.int32, (rows, CHUNK), 1).astype(jnp.float32)
    row = lax.broadcasted_iota(jnp.int32, (rows, CHUNK), 0)
    for c in range(chunks):
        match[0, c] = (by_row == lane + float(c * CHUNK)).astype(jnp.float32)
        match[1, c] = (row == index[:, c * CHUNK : (c + 1) * CHUNK]).astype(jnp.float32)
    acc[...] = jnp.zeros_like(acc)
    total[...] = jnp.zeros_like(total)

    def meet(kind, their_high, their_low, positive):
        both = across(high[kind], jnp.concatenate([their_high, their_low], axis=0))
        dots = both[:, :CHUNK] + both[:, CHUNK:] + across(low[kind], their_high)
        s = scale * dots - 3.0
        e = jnp.exp(-jnp.abs(s))
        weight = jnp.where(s >= 0.0, 1.0, e) / (1.0 + e)
        if positive is not None:
            weight = weight - positive

        @pl.when(kind == 0)
        def _():
            loss = jnp.maximum(s, 0.0) + jnp.log1p(e)
            if positive is not None:
                loss = loss - positive * s
            total[...] += loss

        w_high, w_low = split(scale * weight)
        w_both = jnp.concatenate([w_high, w_low], axis=1)
        for t in range(0, width, 384):
            cut = slice(t, min(t + 384, width))
            top = their_high[:, cut]
            acc[kind, :, cut] += jnp.dot(
                w_both, jnp.concatenate([top, top], axis=0), preferred_element_type=jnp.float32
            ) + jnp.dot(w_high, their_low[:, cut], preferred_element_type=jnp.float32)

    def own_step(n, _):
        c, kind = n // 2, n % 2
        at = pl.ds(pl.multiple_of(c * CHUNK, CHUNK), CHUNK)
        meet(kind, high[1 - kind, at], low[1 - kind, at], match[kind, c])
        return 0

    lax.fori_loop(0, 2 * chunks, own_step, 0)

    def visit(pair_of, kind, c):
        slot = 2 * pair_of + kind
        at = pl.ds(pl.multiple_of(c * CHUNK, CHUNK), CHUNK)
        meet(kind, *split(land[slot, at]), None)

    def early(n, _):
        c, j = n // 4, n % 4
        pair_of = (1 - (j + 2) // 3) * FAR + (j // 3) * NEAR
        second = (j // 2) * (1 - j // 3)
        kind = relayed + second * (odd - relayed)
        for h in range(PARTS):
            q = c * PARTS + h
            arrived(2 * pair_of + kind, q)

            @pl.when(j == 0)
            def _():
                relay(q).start()

        visit(pair_of, kind, c)
        return 0

    lax.fori_loop(0, 4 * chunks, early, 0)

    def store(kind, out):
        return pltpu.make_async_copy(acc.at[kind], out, out_sem.at[kind])

    @pl.when(odd == 0)
    def _():
        store(1, txt_out).start()

    @pl.when(odd == 1)
    def _():
        store(0, img_out).start()

    def late(n, _):
        c, pair_of = n // 2, FAR + n % 2
        for h in range(PARTS):
            arrived(2 * pair_of + odd, c * PARTS + h)
        visit(pair_of, odd, c)
        return 0

    lax.fori_loop(0, 2 * chunks, late, 0)

    @pl.when(odd == 0)
    def _():
        store(0, img_out).start()

    @pl.when(odd == 1)
    def _():
        store(1, txt_out).start()

    loss_row[...] = jnp.sum(jnp.transpose(total[...]), axis=0, keepdims=True) / (4.0 * rows)
    store_loss = pltpu.make_async_copy(loss_row, loss_out, out_sem.at[2])
    store_loss.start()

    def drain(q, _):
        for line, device in enumerate((ahead, behind, partner, lower, upper)):
            send(txt, 0, q, line, device).wait_send()
        relay(q).wait_send()
        return 0

    lax.fori_loop(0, pieces, drain, 0)
    store(0, img_out).wait()
    store(1, txt_out).wait()
    store_loss.wait()


def finish(
    loss, img_part, txt_part, loss_out, img_out, txt_out, row, line, held, in_sem, out_sem
):
    rows = img_part.shape[0]
    step = rows // STRIPS

    def part(n):
        return pl.ds(n * step, step)

    def load(kind, n):
        source = (img_part, txt_part)[kind]
        return pltpu.make_async_copy(
            source.at[part(n)], held.at[kind, part(n)], in_sem.at[1 + kind * STRIPS + n]
        )

    def store(kind, n):
        target = (img_out, txt_out)[kind]
        return pltpu.make_async_copy(
            held.at[kind, part(n)], target.at[part(n)], out_sem.at[1 + kind * STRIPS + n]
        )

    order = [(kind, n) for n in range(STRIPS) for kind in range(2)]
    load_loss = pltpu.make_async_copy(loss, row, in_sem.at[0])
    store_loss = pltpu.make_async_copy(line, loss_out, out_sem.at[0])
    load_loss.start()
    for item in order:
        load(*item).start()
    load_loss.wait()
    line[...] = row[0]
    store_loss.start()
    for item in order:
        load(*item).wait()
        store(*item).start()
    for item in order:
        store(*item).wait()
    store_loss.wait()


def on_device(n_grp, n_blk, images, texts, pair_index):
    rows, width = images.shape
    scale = 2.0 * width ** (-0.5)
    pieces = rows // PIECE
    any_space = pl.BlockSpec(memory_space=pl.ANY)
    limit = 60 * 1024 * 1024
    block = jax.ShapeDtypeStruct((rows, width), jnp.float32)
    loss, image_grad, text_grad = pl.pallas_call(
        functools.partial(kernel, n_grp, n_blk, scale),
        out_shape=(jax.ShapeDtypeStruct((1, rows), jnp.float32), block, block),
        in_specs=[any_space] * 3,
        out_specs=(any_space,) * 3,
        scratch_shapes=[
            pltpu.VMEM((1, rows), jnp.int32),
            pltpu.VMEM((1, rows), jnp.float32),
            pltpu.VMEM((6, rows, width), jnp.float32),
            pltpu.VMEM((2, rows, width), jnp.float32),
            pltpu.VMEM((2, rows, width), jnp.bfloat16),
            pltpu.VMEM((2, rows, width), jnp.bfloat16),
            pltpu.VMEM((2, rows, width), jnp.float32),
            pltpu.VMEM((2, rows // CHUNK, rows, CHUNK), jnp.float32),
            pltpu.VMEM((rows, CHUNK), jnp.float32),
            pltpu.SemaphoreType.DMA((3,)),
            pltpu.SemaphoreType.DMA((3,)),
            pltpu.SemaphoreType.DMA((5, pieces)),
            pltpu.SemaphoreType.DMA((pieces,)),
            pltpu.SemaphoreType.DMA((6, pieces)),
        ],
        compiler_params=pltpu.CompilerParams(
            collective_id=0, has_side_effects=True, vmem_limit_bytes=limit
        ),
        cost_estimate=pl.CostEstimate(
            flops=16 * 3 * 2 * rows * rows * width,
            bytes_accessed=4 * 4 * rows * width,
            transcendentals=8 * rows * rows,
        ),
    )(images, texts, pair_index)
    return pl.pallas_call(
        finish,
        out_shape=(jax.ShapeDtypeStruct((rows,), jnp.float32), block, block),
        in_specs=[any_space] * 3,
        out_specs=(any_space,) * 3,
        scratch_shapes=[
            pltpu.VMEM((1, rows), jnp.float32),
            pltpu.VMEM((rows,), jnp.float32),
            pltpu.VMEM((2, rows, width), jnp.float32),
            pltpu.SemaphoreType.DMA((1 + 2 * STRIPS,)),
            pltpu.SemaphoreType.DMA((1 + 2 * STRIPS,)),
        ],
        compiler_params=pltpu.CompilerParams(vmem_limit_bytes=limit),
        cost_estimate=pl.CostEstimate(
            flops=0, bytes_accessed=4 * 4 * rows * width, transcendentals=0
        ),
    )(loss, image_grad, text_grad)


def solution(mesh):
    n_grp, n_blk = mesh.shape["grp"], mesh.shape["blk"]
    assert n_blk % 2 == 0
    in_specs = (P(("grp", "blk"), None), P(("grp", "blk"), None), P(("grp", "blk"), None))
    out_specs = (P(("grp", "blk")), P(("grp", "blk"), None), P(("grp", "blk"), None))
    return jax.shard_map(
        functools.partial(on_device, n_grp, n_blk),
        mesh=mesh, in_specs=in_specs, out_specs=out_specs, check_vma=False,
    )
```

```python
import functools

import jax
import jax.numpy as jnp
from jax import lax
from jax.experimental import pallas as pl
from jax.experimental.pallas import tpu as pltpu
from jax.sharding import PartitionSpec as P

MESH = pl.DeviceIdType.MESH
CHUNK = 128
PIECE = 64
PARTS = CHUNK // PIECE
HALF = CHUNK // 2
STRIPS = 2

GROUP, FAR, NEAR = 0, 1, 2


def split(value):
    high = value.astype(jnp.bfloat16)
    return high, (value - high.astype(jnp.float32)).astype(jnp.bfloat16)


def across(left, right):
    return lax.dot_general(left, right, (((1,), (1,)), ((), ())), preferred_element_type=jnp.float32)


def kernel(
    n_grp, n_blk, scale,
    img, txt, pair_in, loss_out, img_out, txt_out,
    pair, loss_row, land, own, high, low, acc, match, total,
    own_sem, out_sem, send_sem, relay_sem, recv_sem,
):
    rows, width = img.shape
    pieces = rows // PIECE
    chunks = rows // CHUNK
    g, i = lax.axis_index("grp"), lax.axis_index("blk")
    odd = lax.rem(i, 2)
    relayed = 1 - odd
    partner = (g, i + 1 - 2 * odd)
    ahead, behind = (g, lax.rem(i + 2, n_blk)), (g, lax.rem(i + n_blk - 2, n_blk))
    upper, lower = (lax.rem(g + 1, n_grp), i), (lax.rem(g + n_grp - 1, n_grp), i)

    loads = [
        pltpu.make_async_copy(img, own.at[0], own_sem.at[0]),
        pltpu.make_async_copy(txt, own.at[1], own_sem.at[1]),
        pltpu.make_async_copy(pair_in, pair, own_sem.at[2]),
    ]
    for load in loads:
        load.start()

    barrier = pltpu.get_barrier_semaphore()
    for device in (partner, ahead, behind, upper, lower):
        pl.semaphore_signal(barrier, inc=1, device_id=device, device_id_type=MESH)
    pl.semaphore_wait(barrier, 5)

    def span(q):
        return pl.ds(pl.multiple_of(q * PIECE, PIECE), PIECE)

    def send(src, slot, q, lane, device):
        return pltpu.make_async_remote_copy(
            src_ref=src.at[span(q)],
            dst_ref=land.at[slot, span(q)],
            send_sem=send_sem.at[lane, q],
            recv_sem=recv_sem.at[slot, q],
            device_id=device,
            device_id_type=MESH,
        )

    def relay(q):
        return pltpu.make_async_remote_copy(
            src_ref=land.at[2 * FAR + relayed, span(q)],
            dst_ref=land.at[2 * NEAR + relayed, span(q)],
            send_sem=relay_sem.at[q],
            recv_sem=recv_sem.at[2 * NEAR + relayed, q],
            device_id=partner,
            device_id_type=MESH,
        )

    def arrived(slot, q):
        pltpu.make_async_remote_copy(
            src_ref=land.at[slot, span(q)],
            dst_ref=land.at[slot, span(q)],
            send_sem=relay_sem.at[q],
            recv_sem=recv_sem.at[slot, q],
            device_id=partner,
            device_id_type=MESH,
        ).wait_recv()

    def send_first(q, _):
        @pl.when(odd == 0)
        def _():
            send(img, 2 * FAR + 1, q, 0, behind).start()
            send(txt, 2 * NEAR, q, 2, partner).start()

        @pl.when(odd == 1)
        def _():
            send(txt, 2 * FAR, q, 0, ahead).start()
            send(img, 2 * NEAR + 1, q, 2, partner).start()

        send(txt, 2 * GROUP, q, 3, lower).start()
        return 0

    def send_second(q, _):
        @pl.when(odd == 0)
        def _():
            send(txt, 2 * FAR, q, 1, ahead).start()

        @pl.when(odd == 1)
        def _():
            send(img, 2 * FAR + 1, q, 1, behind).start()

        send(img, 2 * GROUP + 1, q, 4, upper).start()
        return 0

    lax.fori_loop(0, pieces, send_first, 0)
    lax.fori_loop(0, pieces, send_second, 0)

    for load in loads:
        load.wait()
    for kind in range(2):
        for c in range(chunks):
            at = pl.ds(c * CHUNK, CHUNK)
            high[kind, at], low[kind, at] = split(own[kind, at])
    index = pair[...]
    by_row = jnp.transpose(
        jnp.broadcast_to(index.astype(jnp.float32), (CHUNK, rows))
    )
    lane = lax.broadcasted_iota(jnp.int32, (rows, CHUNK), 1).astype(jnp.float32)
    row = lax.broadcasted_iota(jnp.int32, (rows, CHUNK), 0)
    for c in range(chunks):
        match[0, c] = (by_row == lane + float(c * CHUNK)).astype(jnp.float32)
        match[1, c] = (row == index[:, c * CHUNK : (c + 1) * CHUNK]).astype(jnp.float32)
    acc[...] = jnp.zeros_like(acc)
    total[...] = jnp.zeros_like(total)

    def meet(kind, their_high, their_low, positive):
        both = across(high[kind], jnp.concatenate([their_high, their_low], axis=0))
        dots = both[:, :CHUNK] + both[:, CHUNK:] + across(low[kind], their_high)
        s = scale * dots - 3.0
        e = jnp.exp(-jnp.abs(s))
        weight = jnp.where(s >= 0.0, 1.0, e) / (1.0 + e)
        if positive is not None:
            weight = weight - positive

        @pl.when(kind == 0)
        def _():
            loss = jnp.maximum(s, 0.0) + jnp.log1p(e)
            if positive is not None:
                loss = loss - positive * s
            total[...] += loss

        w_high, w_low = split(scale * weight)
        w_both = jnp.concatenate([w_high, w_low], axis=1)
        for t in range(0, width, 384):
            cut = slice(t, min(t + 384, width))
            top = their_high[:, cut]
            acc[kind, :, cut] += jnp.dot(
                w_both, jnp.concatenate([top, top], axis=0), preferred_element_type=jnp.float32
            ) + jnp.dot(w_high, their_low[:, cut], preferred_element_type=jnp.float32)

    def own_step(n, _):
        c, kind = n // 2, n % 2
        at = pl.ds(pl.multiple_of(c * CHUNK, CHUNK), CHUNK)
        meet(kind, high[1 - kind, at], low[1 - kind, at], match[kind, c])
        return 0

    lax.fori_loop(0, 2 * chunks, own_step, 0)

    def visit(pair_of, kind, c):
        slot = 2 * pair_of + kind
        at = pl.ds(pl.multiple_of(c * CHUNK, CHUNK), CHUNK)
        meet(kind, *split(land[slot, at]), None)

    def early(n, _):
        c, j = n // 4, n % 4
        pair_of = (1 - (j + 2) // 3) * FAR + (j // 3) * NEAR
        second = (j // 2) * (1 - j // 3)
        kind = relayed + second * (odd - relayed)
        for h in range(PARTS):
            q = c * PARTS + h
            arrived(2 * pair_of + kind, q)

            @pl.when(j == 0)
            def _():
                relay(q).start()

        visit(pair_of, kind, c)
        return 0

    lax.fori_loop(0, 4 * chunks, early, 0)

    def store(kind, out):
        return pltpu.make_async_copy(acc.at[kind], out, out_sem.at[kind])

    @pl.when(odd == 0)
    def _():
        store(1, txt_out).start()

    @pl.when(odd == 1)
    def _():
        store(0, img_out).start()

    def late(n, _):
        for h in range(PARTS // 2):
            arrived(2 * FAR + odd, n * (PARTS // 2) + h)
            arrived(2 * NEAR + odd, n * (PARTS // 2) + h)
        at = pl.ds(pl.multiple_of(n * HALF, HALF), HALF)
        theirs = jnp.concatenate(
            [land[2 * FAR + odd, at], land[2 * NEAR + odd, at]], axis=0
        )
        meet(odd, *split(theirs), None)
        return 0

    lax.fori_loop(0, 2 * chunks, late, 0)

    @pl.when(odd == 0)
    def _():
        store(0, img_out).start()

    @pl.when(odd == 1)
    def _():
        store(1, txt_out).start()

    loss_row[...] = jnp.sum(jnp.transpose(total[...]), axis=0, keepdims=True) / (4.0 * rows)
    store_loss = pltpu.make_async_copy(loss_row, loss_out, out_sem.at[2])
    store_loss.start()

    def drain(q, _):
        for line, device in enumerate((ahead, behind, partner, lower, upper)):
            send(txt, 0, q, line, device).wait_send()
        relay(q).wait_send()
        return 0

    lax.fori_loop(0, pieces, drain, 0)
    store(0, img_out).wait()
    store(1, txt_out).wait()
    store_loss.wait()


def finish(
    loss, img_part, txt_part, loss_out, img_out, txt_out, row, line, held, in_sem, out_sem
):
    rows = img_part.shape[0]
    step = rows // STRIPS

    def part(n):
        return pl.ds(n * step, step)

    def load(kind, n):
        source = (img_part, txt_part)[kind]
        return pltpu.make_async_copy(
            source.at[part(n)], held.at[kind, part(n)], in_sem.at[1 + kind * STRIPS + n]
        )

    def store(kind, n):
        target = (img_out, txt_out)[kind]
        return pltpu.make_async_copy(
            held.at[kind, part(n)], target.at[part(n)], out_sem.at[1 + kind * STRIPS + n]
        )

    order = [(kind, n) for n in range(STRIPS) for kind in range(2)]
    load_loss = pltpu.make_async_copy(loss, row, in_sem.at[0])
    store_loss = pltpu.make_async_copy(line, loss_out, out_sem.at[0])
    load_loss.start()
    for item in order:
        load(*item).start()
    load_loss.wait()
    line[...] = row[0]
    store_loss.start()
    for item in order:
        load(*item).wait()
        store(*item).start()
    for item in order:
        store(*item).wait()
    store_loss.wait()


def on_device(n_grp, n_blk, images, texts, pair_index):
    rows, width = images.shape
    scale = 2.0 * width ** (-0.5)
    pieces = rows // PIECE
    any_space = pl.BlockSpec(memory_space=pl.ANY)
    limit = 60 * 1024 * 1024
    block = jax.ShapeDtypeStruct((rows, width), jnp.float32)
    loss, image_grad, text_grad = pl.pallas_call(
        functools.partial(kernel, n_grp, n_blk, scale),
        out_shape=(jax.ShapeDtypeStruct((1, rows), jnp.float32), block, block),
        in_specs=[any_space] * 3,
        out_specs=(any_space,) * 3,
        scratch_shapes=[
            pltpu.VMEM((1, rows), jnp.int32),
            pltpu.VMEM((1, rows), jnp.float32),
            pltpu.VMEM((6, rows, width), jnp.float32),
            pltpu.VMEM((2, rows, width), jnp.float32),
            pltpu.VMEM((2, rows, width), jnp.bfloat16),
            pltpu.VMEM((2, rows, width), jnp.bfloat16),
            pltpu.VMEM((2, rows, width), jnp.float32),
            pltpu.VMEM((2, rows // CHUNK, rows, CHUNK), jnp.float32),
            pltpu.VMEM((rows, CHUNK), jnp.float32),
            pltpu.SemaphoreType.DMA((3,)),
            pltpu.SemaphoreType.DMA((3,)),
            pltpu.SemaphoreType.DMA((5, pieces)),
            pltpu.SemaphoreType.DMA((pieces,)),
            pltpu.SemaphoreType.DMA((6, pieces)),
        ],
        compiler_params=pltpu.CompilerParams(
            collective_id=0, has_side_effects=True, vmem_limit_bytes=limit
        ),
        cost_estimate=pl.CostEstimate(
            flops=16 * 3 * 2 * rows * rows * width,
            bytes_accessed=4 * 4 * rows * width,
            transcendentals=8 * rows * rows,
        ),
    )(images, texts, pair_index)
    return pl.pallas_call(
        finish,
        out_shape=(jax.ShapeDtypeStruct((rows,), jnp.float32), block, block),
        in_specs=[any_space] * 3,
        out_specs=(any_space,) * 3,
        scratch_shapes=[
            pltpu.VMEM((1, rows), jnp.float32),
            pltpu.VMEM((rows,), jnp.float32),
            pltpu.VMEM((2, rows, width), jnp.float32),
            pltpu.SemaphoreType.DMA((1 + 2 * STRIPS,)),
            pltpu.SemaphoreType.DMA((1 + 2 * STRIPS,)),
        ],
        compiler_params=pltpu.CompilerParams(vmem_limit_bytes=limit),
        cost_estimate=pl.CostEstimate(
            flops=0, bytes_accessed=4 * 4 * rows * width, transcendentals=0
        ),
    )(loss, image_grad, text_grad)


def solution(mesh):
    n_grp, n_blk = mesh.shape["grp"], mesh.shape["blk"]
    assert n_blk % 2 == 0
    in_specs = (P(("grp", "blk"), None), P(("grp", "blk"), None), P(("grp", "blk"), None))
    out_specs = (P(("grp", "blk")), P(("grp", "blk"), None), P(("grp", "blk"), None))
    return jax.shard_map(
        functools.partial(on_device, n_grp, n_blk),
        mesh=mesh, in_specs=in_specs, out_specs=out_specs, check_vma=False,
    )
```

```python
import functools

import jax
import jax.numpy as jnp
from jax import lax
from jax.experimental import pallas as pl
from jax.experimental.pallas import tpu as pltpu
from jax.sharding import PartitionSpec as P

MESH = pl.DeviceIdType.MESH
CHUNK = 128
PIECE = 64
PARTS = CHUNK // PIECE
HALF = CHUNK // 2
STRIPS = 2

GROUP, FAR, NEAR = 0, 1, 2


def split(value):
    high = value.astype(jnp.bfloat16)
    return high, (value - high.astype(jnp.float32)).astype(jnp.bfloat16)


def across(left, right):
    return lax.dot_general(left, right, (((1,), (1,)), ((), ())), preferred_element_type=jnp.float32)


def kernel(
    n_grp, n_blk, scale,
    img, txt, pair_in, loss_out, img_out, txt_out,
    pair, loss_row, land, own, high, low, acc, match, total,
    own_sem, out_sem, send_sem, relay_sem, recv_sem,
):
    rows, width = img.shape
    pieces = rows // PIECE
    chunks = rows // CHUNK
    g, i = lax.axis_index("grp"), lax.axis_index("blk")
    odd = lax.rem(i, 2)
    relayed = 1 - odd
    partner = (g, i + 1 - 2 * odd)
    ahead, behind = (g, lax.rem(i + 2, n_blk)), (g, lax.rem(i + n_blk - 2, n_blk))
    upper, lower = (lax.rem(g + 1, n_grp), i), (lax.rem(g + n_grp - 1, n_grp), i)

    loads = [
        pltpu.make_async_copy(img, own.at[0], own_sem.at[0]),
        pltpu.make_async_copy(txt, own.at[1], own_sem.at[1]),
        pltpu.make_async_copy(pair_in, pair, own_sem.at[2]),
    ]
    for load in loads:
        load.start()

    barrier = pltpu.get_barrier_semaphore()
    for device in (partner, ahead, behind, upper, lower):
        pl.semaphore_signal(barrier, inc=1, device_id=device, device_id_type=MESH)
    pl.semaphore_wait(barrier, 5)

    def span(q):
        return pl.ds(pl.multiple_of(q * PIECE, PIECE), PIECE)

    def send(src, slot, q, lane, device):
        return pltpu.make_async_remote_copy(
            src_ref=src.at[span(q)],
            dst_ref=land.at[slot, span(q)],
            send_sem=send_sem.at[lane, q],
            recv_sem=recv_sem.at[slot, q],
            device_id=device,
            device_id_type=MESH,
        )

    def relay(q):
        return pltpu.make_async_remote_copy(
            src_ref=land.at[2 * FAR + relayed, span(q)],
            dst_ref=land.at[2 * NEAR + relayed, span(q)],
            send_sem=relay_sem.at[q],
            recv_sem=recv_sem.at[2 * NEAR + relayed, q],
            device_id=partner,
            device_id_type=MESH,
        )

    def arrived(slot, q):
        pltpu.make_async_remote_copy(
            src_ref=land.at[slot, span(q)],
            dst_ref=land.at[slot, span(q)],
            send_sem=relay_sem.at[q],
            recv_sem=recv_sem.at[slot, q],
            device_id=partner,
            device_id_type=MESH,
        ).wait_recv()

    def send_first(q, _):
        @pl.when(odd == 0)
        def _():
            send(img, 2 * FAR + 1, q, 0, behind).start()
            send(txt, 2 * NEAR, q, 2, partner).start()

        @pl.when(odd == 1)
        def _():
            send(txt, 2 * FAR, q, 0, ahead).start()
            send(img, 2 * NEAR + 1, q, 2, partner).start()

        send(txt, 2 * GROUP, q, 3, lower).start()
        return 0

    def send_second(q, _):
        @pl.when(odd == 0)
        def _():
            send(txt, 2 * FAR, q, 1, ahead).start()

        @pl.when(odd == 1)
        def _():
            send(img, 2 * FAR + 1, q, 1, behind).start()

        send(img, 2 * GROUP + 1, q, 4, upper).start()
        return 0

    lax.fori_loop(0, pieces, send_first, 0)
    lax.fori_loop(0, pieces, send_second, 0)

    for load in loads:
        load.wait()
    for kind in range(2):
        for c in range(chunks):
            at = pl.ds(c * CHUNK, CHUNK)
            high[kind, at], low[kind, at] = split(own[kind, at])
    index = pair[...]
    by_row = jnp.transpose(
        jnp.broadcast_to(index.astype(jnp.float32), (CHUNK, rows))
    )
    lane = lax.broadcasted_iota(jnp.int32, (rows, CHUNK), 1).astype(jnp.float32)
    row = lax.broadcasted_iota(jnp.int32, (rows, CHUNK), 0)
    for c in range(chunks):
        match[0, c] = (by_row == lane + float(c * CHUNK)).astype(jnp.float32)
        match[1, c] = (row == index[:, c * CHUNK : (c + 1) * CHUNK]).astype(jnp.float32)
    acc[...] = jnp.zeros_like(acc)
    total[...] = jnp.zeros_like(total)

    def meet(kind, their_high, their_low, positive, leave=None):
        both = across(high[kind], jnp.concatenate([their_high, their_low], axis=0))
        dots = both[:, :CHUNK] + both[:, CHUNK:] + across(low[kind], their_high)
        s = scale * dots - 3.0
        e = jnp.exp(-jnp.abs(s))
        weight = jnp.where(s >= 0.0, 1.0, e) / (1.0 + e)
        if positive is not None:
            weight = weight - positive

        @pl.when(kind == 0)
        def _():
            loss = jnp.maximum(s, 0.0) + jnp.log1p(e)
            if positive is not None:
                loss = loss - positive * s
            total[...] += loss

        w_high, w_low = split(scale * weight)
        w_both = jnp.concatenate([w_high, w_low], axis=1)
        for t in range(0, width, 384):
            cut = slice(t, min(t + 384, width))
            top = their_high[:, cut]
            acc[kind, :, cut] += jnp.dot(
                w_both, jnp.concatenate([top, top], axis=0), preferred_element_type=jnp.float32
            ) + jnp.dot(w_high, their_low[:, cut], preferred_element_type=jnp.float32)
            if leave is not None:
                leave(cut)

    def own_step(n, _):
        c, kind = n // 2, n % 2
        at = pl.ds(pl.multiple_of(c * CHUNK, CHUNK), CHUNK)
        meet(kind, high[1 - kind, at], low[1 - kind, at], match[kind, c])
        return 0

    lax.fori_loop(0, 2 * chunks, own_step, 0)

    def visit(pair_of, kind, c):
        slot = 2 * pair_of + kind
        at = pl.ds(pl.multiple_of(c * CHUNK, CHUNK), CHUNK)
        meet(kind, *split(land[slot, at]), None)

    def early(n, _):
        c, j = n // 4, n % 4
        pair_of = (1 - (j + 2) // 3) * FAR + (j // 3) * NEAR
        second = (j // 2) * (1 - j // 3)
        kind = relayed + second * (odd - relayed)
        for h in range(PARTS):
            q = c * PARTS + h
            arrived(2 * pair_of + kind, q)

            @pl.when(j == 0)
            def _():
                relay(q).start()

        visit(pair_of, kind, c)
        return 0

    lax.fori_loop(0, 4 * chunks, early, 0)

    def store(kind, out):
        return pltpu.make_async_copy(acc.at[kind], out, out_sem.at[kind])

    @pl.when(odd == 0)
    def _():
        store(1, txt_out).start()

    @pl.when(odd == 1)
    def _():
        store(0, img_out).start()

    def leave(cut):
        def strip(kind, out):
            return pltpu.make_async_copy(acc.at[kind, :, cut], out.at[:, cut], out_sem.at[kind])

        @pl.when(odd == 0)
        def _():
            strip(0, img_out).start()

        @pl.when(odd == 1)
        def _():
            strip(1, txt_out).start()

    def late(n, leave=None):
        for h in range(PARTS // 2):
            arrived(2 * FAR + odd, n * (PARTS // 2) + h)
            arrived(2 * NEAR + odd, n * (PARTS // 2) + h)
        at = pl.ds(pl.multiple_of(n * HALF, HALF), HALF)
        theirs = jnp.concatenate(
            [land[2 * FAR + odd, at], land[2 * NEAR + odd, at]], axis=0
        )
        meet(odd, *split(theirs), None, leave)

    @pl.loop(0, 2 * chunks - 1)
    def _(n):
        late(n)

    late(2 * chunks - 1, leave)

    loss_row[...] = jnp.sum(jnp.transpose(total[...]), axis=0, keepdims=True) / (4.0 * rows)
    store_loss = pltpu.make_async_copy(loss_row, loss_out, out_sem.at[2])
    store_loss.start()

    def drain(q, _):
        for line, device in enumerate((ahead, behind, partner, lower, upper)):
            send(txt, 0, q, line, device).wait_send()
        relay(q).wait_send()
        return 0

    lax.fori_loop(0, pieces, drain, 0)
    store(0, img_out).wait()
    store(1, txt_out).wait()
    store_loss.wait()


def finish(
    loss, img_part, txt_part, loss_out, img_out, txt_out, row, line, held, in_sem, out_sem
):
    rows = img_part.shape[0]
    step = rows // STRIPS

    def part(n):
        return pl.ds(n * step, step)

    def load(kind, n):
        source = (img_part, txt_part)[kind]
        return pltpu.make_async_copy(
            source.at[part(n)], held.at[kind, part(n)], in_sem.at[1 + kind * STRIPS + n]
        )

    def store(kind, n):
        target = (img_out, txt_out)[kind]
        return pltpu.make_async_copy(
            held.at[kind, part(n)], target.at[part(n)], out_sem.at[1 + kind * STRIPS + n]
        )

    order = [(kind, n) for n in range(STRIPS) for kind in range(2)]
    load_loss = pltpu.make_async_copy(loss, row, in_sem.at[0])
    store_loss = pltpu.make_async_copy(line, loss_out, out_sem.at[0])
    load_loss.start()
    for item in order:
        load(*item).start()
    load_loss.wait()
    line[...] = row[0]
    store_loss.start()
    for item in order:
        load(*item).wait()
        store(*item).start()
    for item in order:
        store(*item).wait()
    store_loss.wait()


def on_device(n_grp, n_blk, images, texts, pair_index):
    rows, width = images.shape
    scale = 2.0 * width ** (-0.5)
    pieces = rows // PIECE
    any_space = pl.BlockSpec(memory_space=pl.ANY)
    limit = 60 * 1024 * 1024
    block = jax.ShapeDtypeStruct((rows, width), jnp.float32)
    loss, image_grad, text_grad = pl.pallas_call(
        functools.partial(kernel, n_grp, n_blk, scale),
        out_shape=(jax.ShapeDtypeStruct((1, rows), jnp.float32), block, block),
        in_specs=[any_space] * 3,
        out_specs=(any_space,) * 3,
        scratch_shapes=[
            pltpu.VMEM((1, rows), jnp.int32),
            pltpu.VMEM((1, rows), jnp.float32),
            pltpu.VMEM((6, rows, width), jnp.float32),
            pltpu.VMEM((2, rows, width), jnp.float32),
            pltpu.VMEM((2, rows, width), jnp.bfloat16),
            pltpu.VMEM((2, rows, width), jnp.bfloat16),
            pltpu.VMEM((2, rows, width), jnp.float32),
            pltpu.VMEM((2, rows // CHUNK, rows, CHUNK), jnp.float32),
            pltpu.VMEM((rows, CHUNK), jnp.float32),
            pltpu.SemaphoreType.DMA((3,)),
            pltpu.SemaphoreType.DMA((3,)),
            pltpu.SemaphoreType.DMA((5, pieces)),
            pltpu.SemaphoreType.DMA((pieces,)),
            pltpu.SemaphoreType.DMA((6, pieces)),
        ],
        compiler_params=pltpu.CompilerParams(
            collective_id=0, has_side_effects=True, vmem_limit_bytes=limit
        ),
        cost_estimate=pl.CostEstimate(
            flops=16 * 3 * 2 * rows * rows * width,
            bytes_accessed=4 * 4 * rows * width,
            transcendentals=8 * rows * rows,
        ),
    )(images, texts, pair_index)
    return pl.pallas_call(
        finish,
        out_shape=(jax.ShapeDtypeStruct((rows,), jnp.float32), block, block),
        in_specs=[any_space] * 3,
        out_specs=(any_space,) * 3,
        scratch_shapes=[
            pltpu.VMEM((1, rows), jnp.float32),
            pltpu.VMEM((rows,), jnp.float32),
            pltpu.VMEM((2, rows, width), jnp.float32),
            pltpu.SemaphoreType.DMA((1 + 2 * STRIPS,)),
            pltpu.SemaphoreType.DMA((1 + 2 * STRIPS,)),
        ],
        compiler_params=pltpu.CompilerParams(vmem_limit_bytes=limit),
        cost_estimate=pl.CostEstimate(
            flops=0, bytes_accessed=4 * 4 * rows * width, transcendentals=0
        ),
    )(loss, image_grad, text_grad)


def solution(mesh):
    n_grp, n_blk = mesh.shape["grp"], mesh.shape["blk"]
    assert n_blk % 2 == 0
    in_specs = (P(("grp", "blk"), None), P(("grp", "blk"), None), P(("grp", "blk"), None))
    out_specs = (P(("grp", "blk")), P(("grp", "blk"), None), P(("grp", "blk"), None))
    return jax.shard_map(
        functools.partial(on_device, n_grp, n_blk),
        mesh=mesh, in_specs=in_specs, out_specs=out_specs, check_vma=False,
    )
```
